32 devices in a mesh: groups: 2 (over x), wide: 16 (over z, y, core).
Axes of the slice: x: 2, y: 2, z: 4, core: 2. Of those that a mesh axis runs over, the one named last changes fastest.
Arguments:
- features: float32 [196608, 64], P(('groups', 'wide')), parts along dimension 0, may hold values from -6 to 6
- targets: float32 [196608, 128], P(('groups', 'wide')), parts along dimension 0, may hold values from -6 to 6
- block_ids: int32 [4], P('groups'), parts along dimension 0, may hold values from 0 to 95
- order: int32 [196608], P(('groups', 'wide')), parts along dimension 0, may hold values from 0 to 6143, as said below
Outputs:
- coeffs: float32 [196608, 128], P(('groups', 'wide')), parts along dimension 0
- residual: float32 [196608, 128], P(('groups', 'wide')), parts along dimension 0
The draws below stay inside these ranges and needn't reach their ends.
There are 2 independent parts, one for each index of `groups`. The reference program is written for one: setup_inputs(seed, part) draws one part's arguments, and reference() takes and returns one part's arrays. A program takes and returns all parts, laid end to end along the dimension named above; each array names one. Nothing has to cross between parts.
Inputs may be any that keep to these rules, and one draw needn't show every extreme that they name: `order`: each aligned block of 6144 entries starting at a multiple of 6144 is a permutation of 0 .. 6143.
All inputs are finite; a program needn't handle non-finite values.
Results may differ from the reference program's by a relative error of at most 0.0003.
Values sent between devices are 32-bit elements; how exact they have to be, the bound alone decides.
A program may use at most 128 MiB of HBM per device.

```python
import math
import jax
import jax.numpy as jnp
from jax import lax

FEAT = 64
OUT = 128
BLOCK = 1024
STEPS = 2
ROWS_DEV = 6144
POINTS = 98304
NBLOCK = 96


def draw_order(key, part):
    keys = jax.random.split(jax.random.fold_in(key, 17), POINTS // ROWS_DEV)
    rows = jax.vmap(lambda single: jax.random.permutation(single, ROWS_DEV))(keys)
    return rows.reshape(-1).astype(jnp.int32)


def draw_features(key, part):
    base = jax.random.fold_in(key, 23)
    key_scale = jax.random.fold_in(base, 1)
    key_latent = jax.random.fold_in(base, 2)
    key_noise = jax.random.fold_in(base, 3)
    spread = jnp.exp(jax.random.uniform(key_scale, (POINTS, 1), jnp.float32, math.log(0.25), math.log(6.0)))
    latent = jnp.clip(jax.random.normal(key_latent, (POINTS, 6), jnp.float32), -3.0, 3.0)
    columns = jnp.arange(FEAT, dtype=jnp.int32) % 6
    spread_out = jnp.take(latent, columns, axis=1)
    factor = math.sqrt(6.0 / FEAT)
    noise = 0.1 * jax.random.normal(key_noise, (POINTS, FEAT), jnp.float32)
    values = factor * spread * spread_out + noise
    return jnp.clip(values, -6.0, 6.0).astype(jnp.float32)


def levels(stream_key, dims, cuts, least, largest):
    level = 1.0
    for axis_at, parts in cuts:
        heights = jax.random.uniform(jax.random.fold_in(jax.random.fold_in(stream_key, 6), axis_at), (parts,), jnp.float32, least / len(cuts), largest / len(cuts))
        level = level * jnp.repeat(jnp.exp(heights), dims[axis_at] // parts).reshape((-1,) + (1,) * (len(dims) - 1 - axis_at))
    return level


def normal_values(key, extent, deviation, limit, cuts=(), held_as=jnp.bfloat16):
    gain = levels(key, extent, cuts, -0.22, 0.18) if cuts else 1.0
    values = jax.random.normal(key, extent, jnp.float32) * deviation * gain
    return jnp.minimum(jnp.maximum(values, -limit), limit).astype(held_as)


def setup_inputs(seed: int = 0, part: int = 0) -> dict:
    streams_of = jax.random.split(jax.random.key(seed), 5)
    part_keys = jax.random.split(jax.random.fold_in(streams_of[4], part), 5)
    features = draw_features(jax.random.fold_in(jax.random.fold_in(streams_of[4], part), 71), part)
    targets = normal_values(part_keys[1], (POINTS, OUT), 1.0, 6.0, ((0, 16),), jnp.float32)
    block_ids = jax.random.randint(part_keys[2], (STEPS,), 0, NBLOCK).astype(jnp.int32)
    order = draw_order(jax.random.fold_in(jax.random.fold_in(streams_of[4], part), 71), part)
    return {"features": features, "targets": targets, "block_ids": block_ids, "order": order}


def kernel(left, right):
    sq_left = jnp.sum(left * left, axis=1)
    sq_right = jnp.sum(right * right, axis=1)
    cross = jnp.dot(left.astype(jnp.float32), right.T.astype(jnp.float32), precision=lax.Precision.HIGHEST, preferred_element_type=jnp.float32)
    return jnp.exp(-(sq_left[:, None] + sq_right[None, :] - 2.0 * cross) / 32.0)

def factorize(gram):
    half = gram.shape[0] // 2
    top = jnp.linalg.cholesky(gram[:half, :half])
    lower_left = lax.linalg.triangular_solve(top, gram[half:, :half], left_side=False, lower=True, transpose_a=True)
    schur = gram[half:, half:] - jnp.dot(lower_left.astype(jnp.float32), lower_left.T.astype(jnp.float32), precision=lax.Precision.HIGHEST, preferred_element_type=jnp.float32)
    bottom = jnp.linalg.cholesky(schur)
    upper_row = jnp.concatenate([top, jnp.zeros((half, half), dtype=gram.dtype)], axis=1)
    lower_row = jnp.concatenate([lower_left, bottom], axis=1)
    return jnp.concatenate([upper_row, lower_row], axis=0)

def solve_with(factor, right_side):
    halfway = lax.linalg.triangular_solve(factor, right_side, left_side=True, lower=True)
    return lax.linalg.triangular_solve(factor, halfway, left_side=True, lower=True, transpose_a=True)

def reference(features, targets, block_ids, order):
    shards = POINTS // ROWS_DEV
    per = BLOCK // shards
    coeffs = jnp.zeros_like(targets)
    residual = targets
    order_rows = order.reshape(shards, ROWS_DEV)
    feat_shards = features.reshape(shards, ROWS_DEV, FEAT)
    for step in range(STEPS):
        start = (block_ids[step] * per).astype(jnp.int32)
        local = lax.dynamic_slice_in_dim(order_rows, start, per, 1)
        picked = (jnp.arange(shards, dtype=jnp.int32)[:, None] * ROWS_DEV + local).reshape(-1)
        block_x = features[picked]
        block_r = residual[picked]
        gram = kernel(block_x, block_x) + 1.0 * jnp.eye(BLOCK, dtype=jnp.float32)
        factor = factorize(gram)
        delta = solve_with(factor, block_r)
        coeffs = coeffs.at[picked].add(delta)

        def panel(shard_x):
            return jnp.dot(kernel(shard_x, block_x).astype(jnp.float32), delta.astype(jnp.float32), precision=lax.Precision.HIGHEST, preferred_element_type=jnp.float32)
        change = lax.map(panel, feat_shards).reshape(POINTS, OUT)
        residual = residual - change
        residual = residual.at[picked].add(-1.0 * delta)
    return (coeffs, residual)
```

```python
import functools
import math

import jax
import jax.numpy as jnp
from jax import lax
from jax.experimental import pallas as pl
from jax.experimental.pallas import tpu as pltpu
from jax.sharding import PartitionSpec as P

BLOCK = 1024
STEPS = 2
TILE = 256
SQUARINGS = 6
LOG2E = math.log2(math.e)
F32 = jnp.float32
BF16 = jnp.bfloat16
HIGHEST = lax.Precision.HIGHEST
NT = (((1,), (1,)), ((), ()))
NN = (((1,), (0,)), ((), ()))
TN = (((0,), (0,)), ((), ()))


def full(a, b, dims=NN):
    return lax.dot_general(a, b, dims, precision=HIGHEST, preferred_element_type=F32)


def split2(a):
    high = a.astype(BF16)
    return high, (a - high.astype(F32)).astype(BF16)


def three(a, b, dims=NN):
    dot = functools.partial(lax.dot_general, dimension_numbers=dims, preferred_element_type=F32)
    return dot(a[0], b[0]) + (dot(a[0], b[1]) + dot(a[1], b[0]))


def parts3(x):
    xx = jnp.concatenate([x, x], axis=1)
    high = xx.astype(BF16).astype(F32)
    rest = xx - high
    mid = rest.astype(BF16).astype(F32)
    low = rest - mid
    first = lax.broadcasted_iota(jnp.int32, xx.shape, 1) < x.shape[1]
    return high, mid, low, first


def pack_left(x):
    high, mid, low, first = parts3(x)
    return jnp.concatenate(
        [high.astype(BF16), mid.astype(BF16), jnp.where(first, high, low).astype(BF16)], axis=1
    )


def pack_right(x):
    high, mid, low, first = parts3(x)
    both = jnp.where(first, high, mid).astype(BF16)
    return jnp.concatenate([both, both, jnp.where(first, low, high).astype(BF16)], axis=1)


def left_side(x):
    return pack_left(x * (LOG2E / 16.0)), jnp.sum(x * x, axis=1, keepdims=True) * (LOG2E / 32.0)


def gauss(left, left_sq, right, right_sq):
    cross = lax.dot_general(left, right, NT, preferred_element_type=F32)
    return jnp.exp2(cross - left_sq - right_sq)


def bounds_radius():
    low, high = 0.99, TILE + 2.0
    return 2.0 / (low + high), (high - low) / (high + low)


def solve(same, gathered, right, right_sq, gram, weights, inverse, power, rhs, delta):
    shards, rows2, _ = gathered.shape
    per = rows2 // STEPS
    tiles = BLOCK // TILE
    chunk = TILE // per

    def rows_of(system, tile, lanes):
        part = gathered[pl.ds(tile * chunk, chunk), pl.ds(system * per, per), lanes]
        return part.reshape(TILE, part.shape[-1])

    feats = slice(128, 192)
    ones = jnp.ones((8, 64), F32)
    for system in range(STEPS):
        for tile in range(tiles):
            x = rows_of(system, tile, feats)
            at = pl.ds(system * BLOCK + tile * TILE, TILE)
            right[at, :] = pack_right(x)
            right_sq[:, at] = full(ones, x * x, NT) * (LOG2E / 32.0)
            rhs[at, :] = rows_of(system, tile, slice(0, 128))
    eye = (
        lax.broadcasted_iota(jnp.int32, (TILE, TILE), 0)
        == lax.broadcasted_iota(jnp.int32, (TILE, TILE), 1)
    ).astype(F32)
    for system in range(STEPS):
        for tile in range(tiles):
            left, left_sq = left_side(rows_of(system, tile, feats))
            for other in range(tile + 1):
                at = pl.ds(system * BLOCK + other * TILE, TILE)
                value = gauss(left, left_sq, right[at, :], right_sq[0:1, at])
                if other == tile:
                    value = value + 1.0 * eye
                gram[system, tile * TILE : (tile + 1) * TILE, other * TILE : (other + 1) * TILE] = value

    def span(first, last=None):
        return slice(first * TILE, (first + 1 if last is None else last) * TILE)

    def forward(system, k):
        z = rhs[system * BLOCK + k * TILE : system * BLOCK + (k + 1) * TILE, :]
        if k + 1 < tiles:
            at = slice(system * BLOCK + (k + 1) * TILE, (system + 1) * BLOCK)
            rhs[at, :] = rhs[at, :] - full(weights[system, span(k + 1, tiles), span(k)], z)

    def backward(system, k):
        at = slice(system * BLOCK + k * TILE, system * BLOCK + (k + 1) * TILE)
        value = full(inverse[system, k], rhs[at, :])
        if k + 1 < tiles:
            below = delta[system * BLOCK + (k + 1) * TILE : (system + 1) * BLOCK, :]
            value = value - full(weights[system, span(k + 1, tiles), span(k)], below, TN)
        delta[at, :] = value

    for k in range(tiles):
        scale, radius = bounds_radius()
        for system in range(STEPS):
            power[system] = eye - scale * gram[system, span(k), span(k)]
            inverse[system, k] = scale * eye

        def squaring(_, rho):
            square = rho * rho
            step = 2.0 / (2.0 - square)
            for system in range(STEPS):
                e = split2(power[system])
                x = inverse[system, k]
                x_new = step * (x + three(split2(x), e))
                e_new = (1.0 - step) * eye + step * three(e, e)
                inverse[system, k] = x_new
                power[system] = e_new
            return square / (2.0 - square)

        lax.fori_loop(0, SQUARINGS, squaring, jnp.float32(radius))
        for system in range(STEPS):
            x = inverse[system, k]
            error = eye - full(gram[system, span(k), span(k)], x)
            inverse[system, k] = x + three(split2(x), split2(error))
        for system in range(STEPS):
            if k + 1 < tiles:
                below = gram[system, span(k + 1, tiles), span(k)]
                weights[system, span(k + 1, tiles), span(k)] = full(below, inverse[system, k])
        for system in range(STEPS):
            for j in range(k + 1, tiles):
                at = (system, span(j, tiles), span(j))
                gram[at] = gram[at] - full(
                    weights[system, span(j, tiles), span(k)], gram[system, span(j), span(k)], NT
                )
        forward(0, k)
    for k in reversed(range(tiles)):
        backward(0, k)
    delta_one = split2(delta[0:BLOCK, :])
    for tile in range(tiles):
        left, left_sq = left_side(rows_of(1, tile, feats))
        at = slice(BLOCK + tile * TILE, BLOCK + (tile + 1) * TILE)
        cross = gauss(left, left_sq, right[0:BLOCK, :], right_sq[0:1, 0:BLOCK])
        change = three(split2(cross), delta_one) + same * delta[tile * TILE : (tile + 1) * TILE, :]
        rhs[at, :] = rhs[at, :] - change
    for k in range(tiles):
        forward(1, k)
    for k in reversed(range(tiles)):
        backward(1, k)


def kernel(
    scalars, gathered, features, targets, coeffs, residual,
    right, right_sq, gram, weights, inverse, power, rhs, delta, packed,
):
    per = gathered.shape[1] // STEPS
    rows = features.shape[0]
    here = pl.program_id(0)

    @pl.when(here == 0)
    def _():
        me = scalars[STEPS * per]
        same = scalars[STEPS * per + 1].astype(F32)
        solve(same, gathered, right, right_sq, gram, weights, inverse, power, rhs, delta)
        high, low = split2(delta[...])
        packed[...] = jnp.concatenate([high, low], axis=1)
        coeffs[...] = jnp.zeros_like(coeffs)
        for step in range(STEPS):

            def put(j, _):
                row = scalars[step * per + j]
                own = delta[pl.ds(step * BLOCK + me * per + j, 1), :]
                coeffs[pl.ds(row, 1), :] = coeffs[pl.ds(row, 1), :] + own
                return 0

            lax.fori_loop(0, per, put, 0)

    left, left_sq = left_side(features[...])
    width = 512
    total = jnp.zeros((rows, 128), F32)
    for at in range(0, STEPS * BLOCK, width):
        cols = slice(at, at + width)
        value = gauss(left, left_sq, right[cols, :], right_sq[0:1, cols])
        high, low = split2(value)
        wide = jnp.dot(high, packed[cols, :], preferred_element_type=F32)
        narrow = jnp.dot(low, packed[cols, 0:128], preferred_element_type=F32)
        total = total + (wide[:, 0:128] + (wide[:, 128:256] + narrow))
    mine = coeffs[pl.ds(pl.multiple_of(here * rows, rows), rows), :]
    residual[...] = targets[...] - total - mine


def body(features, targets, block_ids, order):
    shards = lax.axis_size("wide")
    me = lax.axis_index("wide").astype(jnp.int32)
    per = BLOCK // shards
    rows_dev, feat = features.shape
    out = targets.shape[1]
    local = jnp.concatenate(
        [lax.dynamic_slice_in_dim(order, block_ids[step] * per, per, 0) for step in range(STEPS)]
    )
    rows = jnp.concatenate([targets[local], features[local]], axis=1)
    gathered = lax.all_gather(rows, "wide", axis=0)
    same = (block_ids[0] == block_ids[1]).astype(jnp.int32)
    scalars = jnp.concatenate([local, jnp.stack([me, same])])
    tile = 512
    grid_spec = pltpu.PrefetchScalarGridSpec(
        num_scalar_prefetch=1,
        grid=(rows_dev // tile,),
        in_specs=[
            pl.BlockSpec((shards, STEPS * per, out + feat), lambda i, s: (0, 0, 0)),
            pl.BlockSpec((tile, feat), lambda i, s: (i, 0)),
            pl.BlockSpec((tile, out), lambda i, s: (i, 0)),
        ],
        out_specs=[
            pl.BlockSpec((rows_dev, out), lambda i, s: (0, 0)),
            pl.BlockSpec((tile, out), lambda i, s: (i, 0)),
        ],
        scratch_shapes=[
            pltpu.VMEM((STEPS * BLOCK, 6 * feat), BF16),
            pltpu.VMEM((8, STEPS * BLOCK), F32),
            pltpu.VMEM((STEPS, BLOCK, BLOCK), F32),
            pltpu.VMEM((STEPS, BLOCK, BLOCK), F32),
            pltpu.VMEM((STEPS, BLOCK // TILE, TILE, TILE), F32),
            pltpu.VMEM((STEPS, TILE, TILE), F32),
            pltpu.VMEM((STEPS * BLOCK, out), F32),
            pltpu.VMEM((STEPS * BLOCK, out), F32),
            pltpu.VMEM((STEPS * BLOCK, 2 * out), BF16),
        ],
    )
    return pl.pallas_call(
        kernel,
        grid_spec=grid_spec,
        out_shape=[jax.ShapeDtypeStruct((rows_dev, out), F32)] * 2,
        compiler_params=pltpu.CompilerParams(
            dimension_semantics=("arbitrary",), vmem_limit_bytes=56 * 1024 * 1024
        ),
        cost_estimate=pl.CostEstimate(
            flops=2 * rows_dev * STEPS * BLOCK * (feat + out) + 2 * STEPS * BLOCK**3,
            bytes_accessed=4 * rows_dev * (feat + 3 * out),
            transcendentals=rows_dev * STEPS * BLOCK,
        ),
        name="block_solve_and_update",
    )(scalars, gathered, features, targets)


def solution(mesh):
    in_specs = (
        P(("groups", "wide"), None),
        P(("groups", "wide"), None),
        P("groups"),
        P(("groups", "wide")),
    )
    out_specs = (P(("groups", "wide"), None), P(("groups", "wide"), None))
    return jax.shard_map(body, mesh=mesh, in_specs=in_specs, out_specs=out_specs, check_vma=False)
```

```python
import functools
import math

import jax
import jax.numpy as jnp
from jax import lax
from jax.experimental import pallas as pl
from jax.experimental.pallas import tpu as pltpu
from jax.sharding import PartitionSpec as P

BLOCK = 1024
STEPS = 2
TILE = 256
SQUARINGS = 6
LOG2E = math.log2(math.e)
F32 = jnp.float32
BF16 = jnp.bfloat16
HIGHEST = lax.Precision.HIGHEST
NT = (((1,), (1,)), ((), ()))
NN = (((1,), (0,)), ((), ()))
TN = (((0,), (0,)), ((), ()))


def full(a, b, dims=NN):
    return lax.dot_general(a, b, dims, precision=HIGHEST, preferred_element_type=F32)


def split2(a):
    high = a.astype(BF16)
    return high, (a - high.astype(F32)).astype(BF16)


def three(a, b, dims=NN):
    dot = functools.partial(lax.dot_general, dimension_numbers=dims, preferred_element_type=F32)
    return dot(a[0], b[0]) + (dot(a[0], b[1]) + dot(a[1], b[0]))


def parts3(x):
    xx = jnp.concatenate([x, x], axis=1)
    high = xx.astype(BF16).astype(F32)
    rest = xx - high
    mid = rest.astype(BF16).astype(F32)
    low = rest - mid
    first = lax.broadcasted_iota(jnp.int32, xx.shape, 1) < x.shape[1]
    return high, mid, low, first


def pack_left(x):
    high, mid, low, first = parts3(x)
    return jnp.concatenate(
        [high.astype(BF16), mid.astype(BF16), jnp.where(first, high, low).astype(BF16)], axis=1
    )


def pack_right(x):
    high, mid, low, first = parts3(x)
    both = jnp.where(first, high, mid).astype(BF16)
    return jnp.concatenate([both, both, jnp.where(first, low, high).astype(BF16)], axis=1)


def left_side(x):
    return pack_left(x * (LOG2E / 16.0)), jnp.sum(x * x, axis=1, keepdims=True) * (LOG2E / 32.0)


def gauss(left, left_sq, right, right_sq):
    cross = lax.dot_general(left, right, NT, preferred_element_type=F32)
    return jnp.exp2(cross - left_sq - right_sq)


def bounds_radius():
    low, high = 0.99, TILE + 2.0
    return 2.0 / (low + high), (high - low) / (high + low)


def tile_of(shared, tile, lanes):
    chunk = TILE // shared.shape[1]
    part = shared[tile * chunk : (tile + 1) * chunk, :, lanes]
    return part.reshape(TILE, part.shape[-1])


def feats_of(shared, system, tile):
    half = shared.shape[2] // STEPS
    return tile_of(shared, tile, slice(system * half, (system + 1) * half))


def span(first, last=None):
    return slice(first * TILE, (first + 1 if last is None else last) * TILE)


def share(shards, x_ref, out_ref, send_near, recv_near, send_far, recv_far, own_sem):
    me = lax.axis_index("wide")
    other = me + 1 - 2 * lax.rem(me, 2)
    half = shards // 2
    barrier = pltpu.get_barrier_semaphore()
    for d in range(1, half):
        pl.semaphore_signal(
            barrier, inc=1, device_id={"wide": lax.rem(me + 2 * d, shards)},
            device_id_type=pl.DeviceIdType.MESH,
        )
    pl.semaphore_signal(
        barrier, inc=1, device_id={"wide": other}, device_id_type=pl.DeviceIdType.MESH
    )
    pl.semaphore_wait(barrier, half)

    own = pltpu.make_async_copy(x_ref, out_ref.at[me], own_sem)
    own.start()
    far = []
    for d in range(1, half):
        copy = pltpu.make_async_remote_copy(
            src_ref=x_ref, dst_ref=out_ref.at[me],
            send_sem=send_far.at[d], recv_sem=recv_far.at[d],
            device_id={"wide": lax.rem(me + 2 * d, shards)},
            device_id_type=pl.DeviceIdType.MESH,
        )
        copy.start()
        far.append(copy)

    def to_other(d, src_ref, slot):
        copy = pltpu.make_async_remote_copy(
            src_ref=src_ref, dst_ref=out_ref.at[slot],
            send_sem=send_near.at[d], recv_sem=recv_near.at[d],
            device_id={"wide": other}, device_id_type=pl.DeviceIdType.MESH,
        )
        copy.start()
        return copy

    near = [to_other(0, x_ref, me)]
    for d in range(1, half):
        far[d - 1].wait_recv()
        slot = lax.rem(me - 2 * d + shards, shards)
        near.append(to_other(d, out_ref.at[slot], slot))
    for copy in far:
        copy.wait_send()
    for copy in near:
        copy.wait()
    own.wait()


def gather_rows(x):
    shards = lax.axis_size("wide")
    half = shards // 2
    return pl.pallas_call(
        functools.partial(share, shards),
        out_shape=jax.ShapeDtypeStruct((shards,) + x.shape, x.dtype),
        in_specs=[pl.BlockSpec(memory_space=pltpu.VMEM)],
        out_specs=pl.BlockSpec(memory_space=pltpu.VMEM),
        scratch_shapes=[pltpu.SemaphoreType.DMA((half,))] * 4 + [pltpu.SemaphoreType.DMA],
        compiler_params=pltpu.CompilerParams(collective_id=0, has_side_effects=True),
        name="share_rows",
    )(x)


def factor(shared, right, right_sq, weights, inverse, gram, power):
    tiles = BLOCK // TILE
    ones = jnp.ones((8, shared.shape[2] // STEPS), F32)
    for system in range(STEPS):
        for tile in range(tiles):
            x = feats_of(shared, system, tile)
            at = slice(system * BLOCK + tile * TILE, system * BLOCK + (tile + 1) * TILE)
            right[at, :] = pack_right(x)
            right_sq[:, at] = full(ones, x * x, NT) * (LOG2E / 32.0)
    eye = (
        lax.broadcasted_iota(jnp.int32, (TILE, TILE), 0)
        == lax.broadcasted_iota(jnp.int32, (TILE, TILE), 1)
    ).astype(F32)
    for system in range(STEPS):
        for tile in range(tiles):
            left, left_sq = left_side(feats_of(shared, system, tile))
            for other in range(tile + 1):
                at = slice(system * BLOCK + other * TILE, system * BLOCK + (other + 1) * TILE)
                value = gauss(left, left_sq, right[at, :], right_sq[0:1, at])
                if other == tile:
                    value = value + 1.0 * eye
                gram[system, span(tile), span(other)] = value

    for k in range(tiles):
        scale, radius = bounds_radius()
        for system in range(STEPS):
            power[system] = eye - scale * gram[system, span(k), span(k)]
            inverse[system, k] = scale * eye

        def squaring(_, rho):
            square = rho * rho
            step = 2.0 / (2.0 - square)
            for system in range(STEPS):
                e = split2(power[system])
                x = inverse[system, k]
                x_new = step * (x + three(split2(x), e))
                e_new = (1.0 - step) * eye + step * three(e, e)
                inverse[system, k] = x_new
                power[system] = e_new
            return square / (2.0 - square)

        lax.fori_loop(0, SQUARINGS, squaring, jnp.float32(radius))
        for system in range(STEPS):
            x = inverse[system, k]
            error = eye - full(gram[system, span(k), span(k)], x)
            inverse[system, k] = x + three(split2(x), split2(error))
        if k + 1 == tiles:
            break
        for system in range(STEPS):
            below = gram[system, span(k + 1, tiles), span(k)]
            weights[system, span(k, tiles - 1), span(k)] = full(below, inverse[system, k])
        for system in range(STEPS):
            for j in range(k + 1, tiles):
                at = (system, span(j, tiles), span(j))
                gram[at] = gram[at] - full(
                    weights[system, span(j - 1, tiles - 1), span(k)],
                    gram[system, span(j), span(k)], NT,
                )


def solve(same, shared, wanted, right, right_sq, weights, inverse, rhs, delta):
    tiles = BLOCK // TILE
    per = shared.shape[1]
    chunk = TILE // per
    for system in range(STEPS):
        for tile in range(tiles):
            part = wanted[tile * chunk : (tile + 1) * chunk, system * per : (system + 1) * per, :]
            at = slice(system * BLOCK + tile * TILE, system * BLOCK + (tile + 1) * TILE)
            rhs[at, :] = part.reshape(TILE, part.shape[-1])

    def forward(system, k):
        if k + 1 < tiles:
            z = rhs[system * BLOCK + k * TILE : system * BLOCK + (k + 1) * TILE, :]
            at = slice(system * BLOCK + (k + 1) * TILE, (system + 1) * BLOCK)
            rhs[at, :] = rhs[at, :] - full(weights[system, span(k, tiles - 1), span(k)], z)

    def backward(system, k):
        at = slice(system * BLOCK + k * TILE, system * BLOCK + (k + 1) * TILE)
        value = full(inverse[system, k], rhs[at, :])
        if k + 1 < tiles:
            below = delta[system * BLOCK + (k + 1) * TILE : (system + 1) * BLOCK, :]
            value = value - full(weights[system, span(k, tiles - 1), span(k)], below, TN)
        delta[at, :] = value

    for k in range(tiles):
        forward(0, k)
    for k in reversed(range(tiles)):
        backward(0, k)
    delta_one = split2(delta[0:BLOCK, :])
    for tile in range(tiles):
        left, left_sq = left_side(feats_of(shared, 1, tile))
        at = slice(BLOCK + tile * TILE, BLOCK + (tile + 1) * TILE)
        cross = gauss(left, left_sq, right[0:BLOCK, :], right_sq[0:1, 0:BLOCK])
        change = three(split2(cross), delta_one) + same * delta[tile * TILE : (tile + 1) * TILE, :]
        rhs[at, :] = rhs[at, :] - change
    for k in range(tiles):
        forward(1, k)
    for k in reversed(range(tiles)):
        backward(1, k)


def update(
    scalars, shared, wanted, right, right_sq, weights, inverse, features, targets,
    coeffs, residual, rhs, delta, packed,
):
    per = shared.shape[1]
    rows = features.shape[0]
    here = pl.program_id(0)

    @pl.when(here == 0)
    def _():
        me = scalars[STEPS * per]
        same = scalars[STEPS * per + 1].astype(F32)
        solve(same, shared, wanted, right, right_sq, weights, inverse, rhs, delta)
        high, low = split2(delta[...])
        packed[...] = jnp.concatenate([high, low], axis=1)
        coeffs[...] = jnp.zeros_like(coeffs)
        for step in range(STEPS):

            def put(j, _):
                row = scalars[step * per + j]
                own = delta[pl.ds(step * BLOCK + me * per + j, 1), :]
                coeffs[pl.ds(row, 1), :] = coeffs[pl.ds(row, 1), :] + own
                return 0

            lax.fori_loop(0, per, put, 0)

    left, left_sq = left_side(features[...])
    width = 512
    total = jnp.zeros((rows, 128), F32)
    for at in range(0, STEPS * BLOCK, width):
        cols = slice(at, at + width)
        value = gauss(left, left_sq, right[cols, :], right_sq[0:1, cols])
        high, low = split2(value)
        wide = jnp.dot(high, packed[cols, :], preferred_element_type=F32)
        narrow = jnp.dot(low, packed[cols, 0:128], preferred_element_type=F32)
        total = total + (wide[:, 0:128] + (wide[:, 128:256] + narrow))
    mine = coeffs[pl.ds(pl.multiple_of(here * rows, rows), rows), :]
    residual[...] = targets[...] - total - mine


def body(features, targets, block_ids, order):
    shards = lax.axis_size("wide")
    me = lax.axis_index("wide").astype(jnp.int32)
    per = BLOCK // shards
    rows_dev, feat = features.shape
    out = targets.shape[1]
    tiles = BLOCK // TILE
    local = jnp.concatenate(
        [lax.dynamic_slice_in_dim(order, block_ids[step] * per, per, 0) for step in range(STEPS)]
    )
    wanted = lax.all_gather(targets[local], "wide", axis=0)
    picked = features[local].reshape(STEPS, per, feat)
    shared = gather_rows(jnp.concatenate([picked[0], picked[1]], axis=1))
    same = (block_ids[0] == block_ids[1]).astype(jnp.int32)
    scalars = jnp.concatenate([local, jnp.stack([me, same])])
    limit = pltpu.CompilerParams(vmem_limit_bytes=56 * 1024 * 1024)
    right, right_sq, weights, inverse = pl.pallas_call(
        factor,
        out_shape=[
            jax.ShapeDtypeStruct((STEPS * BLOCK, 6 * feat), BF16),
            jax.ShapeDtypeStruct((8, STEPS * BLOCK), F32),
            jax.ShapeDtypeStruct((STEPS, BLOCK - TILE, BLOCK - TILE), F32),
            jax.ShapeDtypeStruct((STEPS, tiles, TILE, TILE), F32),
        ],
        scratch_shapes=[
            pltpu.VMEM((STEPS, BLOCK, BLOCK), F32),
            pltpu.VMEM((STEPS, TILE, TILE), F32),
        ],
        compiler_params=limit,
        cost_estimate=pl.CostEstimate(
            flops=24 * STEPS * BLOCK**3, bytes_accessed=16 * BLOCK * BLOCK, transcendentals=0
        ),
        name="factor_blocks",
    )(shared)
    tile = 512

    def whole(array):
        return pl.BlockSpec(array.shape, lambda i, s: (0,) * array.ndim)

    fixed = (shared, wanted, right, right_sq, weights, inverse)
    grid_spec = pltpu.PrefetchScalarGridSpec(
        num_scalar_prefetch=1,
        grid=(rows_dev // tile,),
        in_specs=[whole(array) for array in fixed]
        + [
            pl.BlockSpec((tile, feat), lambda i, s: (i, 0)),
            pl.BlockSpec((tile, out), lambda i, s: (i, 0)),
        ],
        out_specs=[
            pl.BlockSpec((rows_dev, out), lambda i, s: (0, 0)),
            pl.BlockSpec((tile, out), lambda i, s: (i, 0)),
        ],
        scratch_shapes=[
            pltpu.VMEM((STEPS * BLOCK, out), F32),
            pltpu.VMEM((STEPS * BLOCK, out), F32),
            pltpu.VMEM((STEPS * BLOCK, 2 * out), BF16),
        ],
    )
    return pl.pallas_call(
        update,
        grid_spec=grid_spec,
        out_shape=[jax.ShapeDtypeStruct((rows_dev, out), F32)] * 2,
        compiler_params=limit,
        cost_estimate=pl.CostEstimate(
            flops=2 * rows_dev * STEPS * BLOCK * (feat + out),
            bytes_accessed=4 * rows_dev * (feat + 3 * out),
            transcendentals=rows_dev * STEPS * BLOCK,
        ),
        name="solve_and_update",
    )(scalars, *fixed, features, targets)


def solution(mesh):
    in_specs = (
        P(("groups", "wide"), None),
        P(("groups", "wide"), None),
        P("groups"),
        P(("groups", "wide")),
    )
    out_specs = (P(("groups", "wide"), None), P(("groups", "wide"), None))
    return jax.shard_map(body, mesh=mesh, in_specs=in_specs, out_specs=out_specs, check_vma=False)
```

```python
import functools
import math

import jax
import jax.numpy as jnp
from jax import lax
from jax.experimental import pallas as pl
from jax.experimental.pallas import tpu as pltpu
from jax.sharding import PartitionSpec as P

BLOCK = 1024
STEPS = 2
TILE = 256
SQUARINGS = 6
LOG2E = math.log2(math.e)
F32 = jnp.float32
BF16 = jnp.bfloat16
HIGHEST = lax.Precision.HIGHEST
NT = (((1,), (1,)), ((), ()))
NN = (((1,), (0,)), ((), ()))
TN = (((0,), (0,)), ((), ()))


def full(a, b, dims=NN):
    return lax.dot_general(a, b, dims, precision=HIGHEST, preferred_element_type=F32)


def split2(a):
    high = a.astype(BF16)
    return high, (a - high.astype(F32)).astype(BF16)


def three(a, b, dims=NN):
    dot = functools.partial(lax.dot_general, dimension_numbers=dims, preferred_element_type=F32)
    return dot(a[0], b[0]) + (dot(a[0], b[1]) + dot(a[1], b[0]))


def parts3(x):
    xx = jnp.concatenate([x, x], axis=1)
    high = xx.astype(BF16).astype(F32)
    rest = xx - high
    mid = rest.astype(BF16).astype(F32)
    low = rest - mid
    first = lax.broadcasted_iota(jnp.int32, xx.shape, 1) < x.shape[1]
    return high, mid, low, first


def norm_chunk(square, first_lane, other_lane, sign):
    high = square.astype(BF16).astype(F32)
    rest = square - high
    mid = rest.astype(BF16).astype(F32)
    lane = lax.broadcasted_iota(jnp.int32, (square.shape[0], 128), 1)
    terms = jnp.where(lane == first_lane, high, jnp.where(lane == first_lane + 1, mid, rest - mid))
    inside = (lane >= first_lane) & (lane < first_lane + 3)
    other = (lane >= other_lane) & (lane < other_lane + 3)
    return jnp.where(inside, sign * terms, jnp.where(other, 1.0 * sign, 0.0)).astype(BF16)


def squares(x):
    return jnp.sum(x * x, axis=1, keepdims=True) * (LOG2E / 32.0)


def pack_left(x):
    high, mid, low, first = parts3(x * (LOG2E / 16.0))
    cross = jnp.where(first, high, low).astype(BF16)
    norm = norm_chunk(squares(x), 0, 3, 1.0)
    return jnp.concatenate([high.astype(BF16), mid.astype(BF16), cross, norm], axis=1)


def pack_right(x):
    high, mid, low, first = parts3(x)
    both = jnp.where(first, high, mid).astype(BF16)
    cross = jnp.where(first, low, high).astype(BF16)
    norm = norm_chunk(squares(x), 3, 0, -1.0)
    return jnp.concatenate([both, both, cross, norm], axis=1)


def gauss(left, right):
    return jnp.exp2(lax.dot_general(left, right, NT, preferred_element_type=F32))


def bounds_radius():
    low, high = 0.99, TILE + 2.0
    return 2.0 / (low + high), (high - low) / (high + low)


def tile_of(shared, tile, lanes):
    chunk = TILE // shared.shape[1]
    part = shared[tile * chunk : (tile + 1) * chunk, :, lanes]
    return part.reshape(TILE, part.shape[-1])


def feats_of(shared, system, tile):
    half = shared.shape[2] // STEPS
    return tile_of(shared, tile, slice(system * half, (system + 1) * half))


def span(first, last=None):
    return slice(first * TILE, (first + 1 if last is None else last) * TILE)


def share(shards, x_ref, out_ref, send_near, recv_near, send_far, recv_far, own_sem):
    me = lax.axis_index("wide")
    other = me + 1 - 2 * lax.rem(me, 2)
    half = shards // 2
    barrier = pltpu.get_barrier_semaphore()
    for d in range(1, half):
        pl.semaphore_signal(
            barrier, inc=1, device_id={"wide": lax.rem(me + 2 * d, shards)},
            device_id_type=pl.DeviceIdType.MESH,
        )
    pl.semaphore_signal(
        barrier, inc=1, device_id={"wide": other}, device_id_type=pl.DeviceIdType.MESH
    )
    pl.semaphore_wait(barrier, half)

    own = pltpu.make_async_copy(x_ref, out_ref.at[me], own_sem)
    own.start()
    far = []
    for d in range(1, half):
        copy = pltpu.make_async_remote_copy(
            src_ref=x_ref, dst_ref=out_ref.at[me],
            send_sem=send_far.at[d], recv_sem=recv_far.at[d],
            device_id={"wide": lax.rem(me + 2 * d, shards)},
            device_id_type=pl.DeviceIdType.MESH,
        )
        copy.start()
        far.append(copy)

    def to_other(d, src_ref, slot):
        copy = pltpu.make_async_remote_copy(
            src_ref=src_ref, dst_ref=out_ref.at[slot],
            send_sem=send_near.at[d], recv_sem=recv_near.at[d],
            device_id={"wide": other}, device_id_type=pl.DeviceIdType.MESH,
        )
        copy.start()
        return copy

    near = [to_other(0, x_ref, me)]
    for d in range(1, half):
        far[d - 1].wait_recv()
        slot = lax.rem(me - 2 * d + shards, shards)
        near.append(to_other(d, out_ref.at[slot], slot))
    for copy in far:
        copy.wait_send()
    for copy in near:
        copy.wait()
    own.wait()


def gather_rows(x):
    shards = lax.axis_size("wide")
    half = shards // 2
    return pl.pallas_call(
        functools.partial(share, shards),
        out_shape=jax.ShapeDtypeStruct((shards,) + x.shape, x.dtype),
        in_specs=[pl.BlockSpec(memory_space=pltpu.VMEM)],
        out_specs=pl.BlockSpec(memory_space=pltpu.VMEM),
        scratch_shapes=[pltpu.SemaphoreType.DMA((half,))] * 4 + [pltpu.SemaphoreType.DMA],
        compiler_params=pltpu.CompilerParams(collective_id=0, has_side_effects=True),
        name="share_rows",
    )(x)


def factor(shared, right, weights, inverse, gram, power):
    tiles = BLOCK // TILE
    for system in range(STEPS):
        for tile in range(tiles):
            x = feats_of(shared, system, tile)
            at = slice(system * BLOCK + tile * TILE, system * BLOCK + (tile + 1) * TILE)
            right[at, :] = pack_right(x)
    eye = (
        lax.broadcasted_iota(jnp.int32, (TILE, TILE), 0)
        == lax.broadcasted_iota(jnp.int32, (TILE, TILE), 1)
    ).astype(F32)
    for system in range(STEPS):
        for tile in range(tiles):
            left = pack_left(feats_of(shared, system, tile))
            for other in range(tile + 1):
                at = slice(system * BLOCK + other * TILE, system * BLOCK + (other + 1) * TILE)
                value = gauss(left, right[at, :])
                if other == tile:
                    value = value + 1.0 * eye
                gram[system, span(tile), span(other)] = value

    for k in range(tiles):
        scale, radius = bounds_radius()
        for system in range(STEPS):
            power[system] = eye - scale * gram[system, span(k), span(k)]
            inverse[system, k] = scale * eye

        def squaring(_, rho):
            square = rho * rho
            step = 2.0 / (2.0 - square)
            for system in range(STEPS):
                x = inverse[system, k]
                high, low = split2(jnp.concatenate([power[system], x], axis=0))
                product = three((high, low), (high[0:TILE], low[0:TILE]))
                inverse[system, k] = step * (x + product[TILE:])
                power[system] = (1.0 - step) * eye + step * product[0:TILE]
            return square / (2.0 - square)

        lax.fori_loop(0, SQUARINGS, squaring, jnp.float32(radius))
        for system in range(STEPS):
            x = inverse[system, k]
            error = eye - full(gram[system, span(k), span(k)], x)
            inverse[system, k] = x + three(split2(x), split2(error))
        if k + 1 == tiles:
            break
        for system in range(STEPS):
            below = gram[system, span(k + 1, tiles), span(k)]
            weights[system, span(k, tiles - 1), span(k)] = full(below, inverse[system, k])
        for system in range(STEPS):
            for j in range(k + 1, tiles):
                at = (system, span(j, tiles), span(j))
                gram[at] = gram[at] - full(
                    weights[system, span(j - 1, tiles - 1), span(k)],
                    gram[system, span(j), span(k)], NT,
                )


def solve(same, shared, wanted, right, weights, inverse, rhs, delta):
    tiles = BLOCK // TILE
    per = shared.shape[1]
    chunk = TILE // per
    for system in range(STEPS):
        for tile in range(tiles):
            part = wanted[tile * chunk : (tile + 1) * chunk, system * per : (system + 1) * per, :]
            at = slice(system * BLOCK + tile * TILE, system * BLOCK + (tile + 1) * TILE)
            rhs[at, :] = part.reshape(TILE, part.shape[-1])

    def forward(system, k):
        if k + 1 < tiles:
            z = rhs[system * BLOCK + k * TILE : system * BLOCK + (k + 1) * TILE, :]
            at = slice(system * BLOCK + (k + 1) * TILE, (system + 1) * BLOCK)
            rhs[at, :] = rhs[at, :] - full(weights[system, span(k, tiles - 1), span(k)], z)

    def backward(system, k):
        at = slice(system * BLOCK + k * TILE, system * BLOCK + (k + 1) * TILE)
        value = full(inverse[system, k], rhs[at, :])
        if k + 1 < tiles:
            below = delta[system * BLOCK + (k + 1) * TILE : (system + 1) * BLOCK, :]
            value = value - full(weights[system, span(k, tiles - 1), span(k)], below, TN)
        delta[at, :] = value

    for k in range(tiles):
        forward(0, k)
    for k in reversed(range(tiles)):
        backward(0, k)
    delta_one = split2(delta[0:BLOCK, :])
    for tile in range(tiles):
        left = pack_left(feats_of(shared, 1, tile))
        at = slice(BLOCK + tile * TILE, BLOCK + (tile + 1) * TILE)
        cross = gauss(left, right[0:BLOCK, :])
        change = three(split2(cross), delta_one) + same * delta[tile * TILE : (tile + 1) * TILE, :]
        rhs[at, :] = rhs[at, :] - change
    for k in range(tiles):
        forward(1, k)
    for k in reversed(range(tiles)):
        backward(1, k)


def update(
    scalars, shared, wanted, right, weights, inverse, features, targets,
    coeffs, residual, rhs, delta, packed,
):
    per = shared.shape[1]
    rows = features.shape[0]
    here = pl.program_id(0)

    @pl.when(here == 0)
    def _():
        me = scalars[STEPS * per]
        same = scalars[STEPS * per + 1].astype(F32)
        solve(same, shared, wanted, right, weights, inverse, rhs, delta)
        high, low = split2(delta[...])
        packed[...] = jnp.concatenate([high, low], axis=1)
        coeffs[...] = jnp.zeros_like(coeffs)
        for step in range(STEPS):

            def put(j, _):
                row = scalars[step * per + j]
                own = delta[pl.ds(step * BLOCK + me * per + j, 1), :]
                coeffs[pl.ds(row, 1), :] = coeffs[pl.ds(row, 1), :] + own
                return 0

            lax.fori_loop(0, per, put, 0)

    left = pack_left(features[...])
    width = 512
    total = jnp.zeros((rows, 128), F32)
    for at in range(0, STEPS * BLOCK, width):
        cols = slice(at, at + width)
        value = gauss(left, right[cols, :])
        high, low = split2(value)
        wide = jnp.dot(high, packed[cols, :], preferred_element_type=F32)
        narrow = jnp.dot(low, packed[cols, 0:128], preferred_element_type=F32)
        total = total + (wide[:, 0:128] + (wide[:, 128:256] + narrow))
    mine = coeffs[pl.ds(pl.multiple_of(here * rows, rows), rows), :]
    residual[...] = targets[...] - total - mine


def body(features, targets, block_ids, order):
    shards = lax.axis_size("wide")
    me = lax.axis_index("wide").astype(jnp.int32)
    per = BLOCK // shards
    rows_dev, feat = features.shape
    out = targets.shape[1]
    tiles = BLOCK // TILE
    local = jnp.concatenate(
        [lax.dynamic_slice_in_dim(order, block_ids[step] * per, per, 0) for step in range(STEPS)]
    )
    wanted = lax.all_gather(targets[local], "wide", axis=0)
    picked = features[local].reshape(STEPS, per, feat)
    shared = gather_rows(jnp.concatenate([picked[0], picked[1]], axis=1))
    same = (block_ids[0] == block_ids[1]).astype(jnp.int32)
    scalars = jnp.concatenate([local, jnp.stack([me, same])])
    limit = pltpu.CompilerParams(vmem_limit_bytes=56 * 1024 * 1024)
    right, weights, inverse = pl.pallas_call(
        factor,
        out_shape=[
            jax.ShapeDtypeStruct((STEPS * BLOCK, 8 * feat), BF16),
            jax.ShapeDtypeStruct((STEPS, BLOCK - TILE, BLOCK - TILE), F32),
            jax.ShapeDtypeStruct((STEPS, tiles, TILE, TILE), F32),
        ],
        scratch_shapes=[
            pltpu.VMEM((STEPS, BLOCK, BLOCK), F32),
            pltpu.VMEM((STEPS, TILE, TILE), F32),
        ],
        compiler_params=limit,
        cost_estimate=pl.CostEstimate(
            flops=24 * STEPS * BLOCK**3, bytes_accessed=16 * BLOCK * BLOCK, transcendentals=0
        ),
        name="factor_blocks",
    )(shared)
    tile = 512

    def whole(array):
        return pl.BlockSpec(array.shape, lambda i, s: (0,) * array.ndim)

    fixed = (shared, wanted, right, weights, inverse)
    grid_spec = pltpu.PrefetchScalarGridSpec(
        num_scalar_prefetch=1,
        grid=(rows_dev // tile,),
        in_specs=[whole(array) for array in fixed]
        + [
            pl.BlockSpec((tile, feat), lambda i, s: (i, 0)),
            pl.BlockSpec((tile, out), lambda i, s: (i, 0)),
        ],
        out_specs=[
            pl.BlockSpec((rows_dev, out), lambda i, s: (0, 0)),
            pl.BlockSpec((tile, out), lambda i, s: (i, 0)),
        ],
        scratch_shapes=[
            pltpu.VMEM((STEPS * BLOCK, out), F32),
            pltpu.VMEM((STEPS * BLOCK, out), F32),
            pltpu.VMEM((STEPS * BLOCK, 2 * out), BF16),
        ],
    )
    return pl.pallas_call(
        update,
        grid_spec=grid_spec,
        out_shape=[jax.ShapeDtypeStruct((rows_dev, out), F32)] * 2,
        compiler_params=limit,
        cost_estimate=pl.CostEstimate(
            flops=2 * rows_dev * STEPS * BLOCK * (feat + out),
            bytes_accessed=4 * rows_dev * (feat + 3 * out),
            transcendentals=rows_dev * STEPS * BLOCK,
        ),
        name="solve_and_update",
    )(scalars, *fixed, features, targets)


def solution(mesh):
    in_specs = (
        P(("groups", "wide"), None),
        P(("groups", "wide"), None),
        P("groups"),
        P(("groups", "wide")),
    )
    out_specs = (P(("groups", "wide"), None), P(("groups", "wide"), None))
    return jax.shard_map(body, mesh=mesh, in_specs=in_specs, out_specs=out_specs, check_vma=False)
```
